128 devices in a mesh: dp: 8 (over y, core), fsdp: 16 (over x, z).
Axes of the slice: x: 4, y: 4, z: 4, core: 2. Of those that a mesh axis runs over, the one named last changes fastest.
Arguments:
- hidden: bfloat16 [8192, 14784], P('fsdp', 'dp'), may hold values from -6 to 6
- cotangent: bfloat16 [8192, 8192], P('fsdp', 'dp'), may hold values from -6 to 6
- down_weight: bfloat16 [14784, 8192], P('dp', 'fsdp'), may hold values from -0.046875 to 0.046875
- adapter_in: bfloat16 [16, 64, 14784], P(None, None, 'dp'), may hold values from -0.046875 to 0.046875
- adapter_out: bfloat16 [16, 64, 8192], P(None, None, 'dp'), may hold values from -0.0625 to 0.0625
- adapter_ids: int32 [64, 1], P('fsdp'), may hold values from 0 to 15
- adapter_slot: int32 [16], replicated, may hold values from 0 to 15, each once
Outputs:
- hidden_gradient: bfloat16 [8192, 14784], P('fsdp', 'dp')
- grad_in: bfloat16 [16, 64, 14784], P('fsdp', None, 'dp')
- grad_out: bfloat16 [16, 64, 8192], P('fsdp', None, 'dp')
The draws below stay inside these ranges and needn't reach their ends.
Inputs may be any that keep to these rules, and one draw needn't show every extreme that they name: `adapter_ids`: every adapter is named by at least one block. A permutation; adapter a's weights and gradients stand at slot adapter_slot[a].
All inputs are finite; a program needn't handle non-finite values.
Results may differ from the reference program's by a relative error of at most 0.025.
Values may be sent and summed in bfloat16 or wider, within the bound.
No kernel may reach another device: no remote copies, remote signals or barrier semaphores. Data moves between devices by JAX's collectives and lax.ppermute only.
A program may use at most 192 MiB of HBM per device.

```python
import math
import jax
import jax.numpy as jnp
from jax import lax

D = 8192
FF = 14784
R = 64
BLOCK = 128
TOKENS_PER_SHARD = 512
TOKENS = 8192
BLOCKS = 64
ADAPTERS = 16
N_FSDP = 16


def block_levels(own_key, extent, cuts, least, high):
    factor_of, own = 1.0, jax.random.fold_in(own_key, 6)
    for axis_at, blocks in cuts:
        heights = jnp.exp(jax.random.uniform(jax.random.fold_in(own, axis_at), (blocks,), jnp.float32, least / len(cuts), high / len(cuts)))
        factor_of = factor_of * jnp.repeat(heights, extent[axis_at] // blocks).reshape([-1 if axis == axis_at else 1 for axis in range(len(extent))])
    return factor_of


def distinct(own_key, rows, amount, top, lift):
    order = jax.random.permutation(jax.random.fold_in(own_key, 1), amount)
    favour = order
    for power in range(3):
        favour = favour * favour // amount
    favour = favour * lift // amount
    lots = jax.random.randint(jax.random.fold_in(own_key, 2), (rows, amount), 0, 4096) + favour
    sure = jax.random.permutation(jax.random.fold_in(own_key, 3), rows)[jnp.arange(amount) % rows]
    lots = jnp.where(jnp.arange(rows)[:, None] == sure[None, :], 1 << 14, lots)
    score = lots * amount + jnp.arange(amount)
    return lax.top_k(score.astype(jnp.int32), top)[1].astype(jnp.int32)


def noise(key, shape, width, most, shards=(), kind=jnp.bfloat16):
    gain = block_levels(key, shape, shards, -0.22, 0.18) if shards else 1.0
    values = jax.random.normal(key, shape, jnp.float32) * width * gain
    return jnp.minimum(jnp.maximum(values, -most), most).astype(kind)


def setup_inputs(seed: int = 0) -> dict:
    arg_keys = jax.random.split(jax.random.key(seed), 8)
    return {
        "hidden": noise(arg_keys[0], (TOKENS, FF), 1.0, 6.0, ((0, 16), (1, 8))),
        "cotangent": noise(arg_keys[1], (TOKENS, D), 1.0, 6.0, ((0, 16), (1, 8))),
        "down_weight": noise(arg_keys[2], (FF, D), FF ** -0.5, 0.046875, ((0, 8), (1, 16))),
        "adapter_in": noise(arg_keys[3], (ADAPTERS, R, FF), FF ** -0.5, 0.046875, ((2, 8),)),
        "adapter_out": noise(arg_keys[4], (ADAPTERS, R, D), D ** -0.5, 0.0625, ((2, 8),)),
        "adapter_ids": distinct(arg_keys[5], BLOCKS, ADAPTERS, 1, 1024),
        "adapter_slot": jax.random.permutation(arg_keys[6], ADAPTERS).astype(jnp.int32),
    }


adapter_scale = 2.0

def reference(hidden, cotangent, down_weight, adapter_in, adapter_out, adapter_ids, adapter_slot):
    block_count = hidden.shape[0] // BLOCK
    slot_index = adapter_slot[adapter_ids[:, 0]].astype(jnp.int32)
    frozen_path_gradient = lax.dot_general(cotangent, down_weight, (((1,), (1,)), ((), ())), preferred_element_type=jnp.float32)
    chosen_in = adapter_in[slot_index].astype(jnp.float32)
    chosen_out = adapter_out[slot_index].astype(jnp.float32)
    hidden_blocks = hidden.reshape(block_count, BLOCK, FF).astype(jnp.float32)
    cotangent_blocks = cotangent.reshape(block_count, BLOCK, D).astype(jnp.float32)
    project = jnp.einsum('btd,brd->btr', cotangent_blocks, chosen_out).astype(jnp.bfloat16)
    reduced = jnp.einsum('btf,brf->btr', hidden_blocks, chosen_in).astype(jnp.bfloat16)
    project_wide = project.astype(jnp.float32)
    reduced_wide = reduced.astype(jnp.float32)
    reduced_rank_product = jnp.einsum('btr,brf->btf', project_wide, chosen_in).reshape(block_count * BLOCK, FF)
    hidden_gradient = (frozen_path_gradient + adapter_scale * reduced_rank_product).astype(jnp.bfloat16)
    adapter_multiplier = adapter_scale / math.sqrt(TOKENS_PER_SHARD)
    block_in = jnp.einsum('btr,btf->brf', project_wide, hidden_blocks) * adapter_multiplier
    block_out = jnp.einsum('btr,btd->brd', reduced_wide, cotangent_blocks) * adapter_multiplier
    onehot = (slot_index[:, None] == jnp.arange(ADAPTERS, dtype=jnp.int32)[None, :]).astype(jnp.float32)
    device_blocks = block_count // N_FSDP

    def accumulate(totals, device):
        offset = (device * device_blocks).astype(jnp.int32)
        chosen = lax.dynamic_slice_in_dim(onehot, offset, device_blocks, 0)
        piece_in = lax.dynamic_slice_in_dim(block_in, offset, device_blocks, 0)
        piece_out = lax.dynamic_slice_in_dim(block_out, offset, device_blocks, 0)
        partial_in = jnp.einsum('ba,brf->arf', chosen, piece_in, precision=lax.Precision.HIGHEST)
        partial_out = jnp.einsum('ba,brd->ard', chosen, piece_out, precision=lax.Precision.HIGHEST)
        partial_in = lax.optimization_barrier(partial_in.astype(jnp.bfloat16))
        partial_out = lax.optimization_barrier(partial_out.astype(jnp.bfloat16))
        return ((totals[0] + partial_in.astype(jnp.float32), totals[1] + partial_out.astype(jnp.float32)), None)
    initial = (jnp.zeros((ADAPTERS, R, FF), jnp.float32), jnp.zeros((ADAPTERS, R, D), jnp.float32))
    totals, unused = lax.scan(accumulate, initial, jnp.arange(N_FSDP, dtype=jnp.int32))
    return (hidden_gradient, totals[0].astype(jnp.bfloat16), totals[1].astype(jnp.bfloat16))
```

```python
import math

import jax
import jax.numpy as jnp
from jax import lax
from jax.experimental import pallas as pl
from jax.experimental.pallas import tpu as pltpu
from jax.sharding import Mesh, PartitionSpec as P

adapter_scale = 2.0
N = 4
CHUNKS = (896, 952)
VMEM = 48 * 1024 * 1024
CONTRACT_LAST = (((1,), (1,)), ((), ()))
CONTRACT_FIRST = (((0,), (0,)), ((), ()))


def take_from(array, axis, step):
    return lax.ppermute(array, axis, [((i + step) % N, i) for i in range(N)])


def other_core(array):
    return lax.ppermute(array, "c", [(0, 1), (1, 0)])


def sum_over_dp(array):
    array = array + other_core(array)
    array = array + lax.ppermute(array, "y", [(0, 1), (1, 0), (2, 3), (3, 2)])
    return array + lax.ppermute(array, "y", [(0, 3), (3, 0), (1, 2), (2, 1)])


def gather_ring(array, axis, cut_axis):
    after = take_from(array, axis, 1)
    before = take_from(array, axis, -1)
    half = array.shape[cut_axis] // 2
    far_low = take_from(lax.slice_in_dim(after, 0, half, axis=cut_axis), axis, 1)
    far_high = take_from(lax.slice_in_dim(before, half, 2 * half, axis=cut_axis), axis, -1)
    return after, before, far_low, far_high


def whole(array):
    return pl.BlockSpec(array.shape, lambda i, ix: (0,) * array.ndim)


def rank_kernel(slots, cotangent, hidden, a_out, a_in, out):
    rank = a_out.shape[1]
    out[:, :rank] = lax.dot_general(
        cotangent[...], a_out[0], CONTRACT_LAST, preferred_element_type=jnp.float32
    ).astype(out.dtype)
    out[:, rank:] = lax.dot_general(
        hidden[...], a_in[0], CONTRACT_LAST, preferred_element_type=jnp.float32
    ).astype(out.dtype)


def rank_sums(slots, cotangent, hidden, adapter_out, adapter_in):
    tokens, width = cotangent.shape
    units = hidden.shape[1]
    rank = adapter_in.shape[1]
    blocks = slots.shape[0]
    rows = tokens // blocks
    return pl.pallas_call(
        rank_kernel,
        grid_spec=pltpu.PrefetchScalarGridSpec(
            num_scalar_prefetch=1,
            grid=(blocks,),
            in_specs=[
                pl.BlockSpec((rows, width), lambda i, s: (i, 0)),
                pl.BlockSpec((rows, units), lambda i, s: (i, 0)),
                pl.BlockSpec((1, rank, width), lambda i, s: (s[i], 0, 0)),
                pl.BlockSpec((1, rank, units), lambda i, s: (s[i], 0, 0)),
            ],
            out_specs=pl.BlockSpec((rows, 2 * rank), lambda i, s: (i, 0)),
        ),
        out_shape=jax.ShapeDtypeStruct((tokens, 2 * rank), jnp.bfloat16),
        compiler_params=pltpu.CompilerParams(vmem_limit_bytes=VMEM),
    )(slots, cotangent, hidden, adapter_out, adapter_in)


def terms_kernel(multiplier, index, summed, cotangent, hidden, *refs):
    outs, products = refs[:7], refs[7]
    blocks = products.shape[0]
    rows = cotangent.shape[0] // blocks
    width = cotangent.shape[1]
    rank = summed.shape[1] // 2
    for b in range(blocks):
        at = slice(b * rows, (b + 1) * rows)
        products[b, :, :width] = lax.dot_general(
            summed[at, rank:], cotangent[at, :], CONTRACT_FIRST, preferred_element_type=jnp.float32
        )
        products[b, :, width:] = lax.dot_general(
            summed[at, :rank], hidden[at, :], CONTRACT_FIRST, preferred_element_type=jnp.float32
        )
    x, z = index[blocks], index[blocks + 1]
    place = 0
    for s in (2, 1, 3, 0):
        for half in range(2):
            ref = outs[place] if s else outs[6]
            for low in range(2):
                t = (2, 1, 3, 0)[half * 2 + low]
                slot = lax.rem(x + s, N) * N + lax.rem(z + t, N)
                total = jnp.zeros(products.shape[1:], jnp.float32)
                for b in range(blocks):
                    weight = jnp.where(index[b] == slot, jnp.float32(multiplier), jnp.float32(0))
                    total = total + weight * products[b]
                row = (low if s else half * 2 + low) * rank
                ref[row : row + rank, :] = total.astype(ref.dtype)
            place += 1


def gradient_terms(slots, x, z, summed, cotangent, hidden, multiplier):
    blocks = slots.shape[0]
    wide = cotangent.shape[1] + hidden.shape[1]
    rank = summed.shape[1] // 2
    shapes = [(2 * rank, wide)] * 6 + [(4 * rank, wide)]
    index = jnp.concatenate([slots, jnp.stack([x, z]).astype(jnp.int32)])

    def kernel(*refs):
        terms_kernel(multiplier, *refs)

    return pl.pallas_call(
        kernel,
        grid_spec=pltpu.PrefetchScalarGridSpec(
            num_scalar_prefetch=1,
            grid=(1,),
            in_specs=[whole(a) for a in (summed, cotangent, hidden)],
            out_specs=[pl.BlockSpec(s, lambda i, ix: (0, 0)) for s in shapes],
            scratch_shapes=[pltpu.VMEM((blocks, rank, wide), jnp.float32)],
        ),
        out_shape=[jax.ShapeDtypeStruct(s, jnp.bfloat16) for s in shapes],
        compiler_params=pltpu.CompilerParams(vmem_limit_bytes=VMEM),
    )(index, summed, cotangent, hidden)


def product_kernel(even, index, mine, other, w0, w1, w3, w2a, w2b, *refs):
    outs, (wide, rows) = refs[:-2], refs[-2:]
    step = pl.program_id(0)
    x, y = index[2], index[3]
    width = w0.shape[1]

    @pl.when(step == 0)
    def _():
        for r, piece in ((0, w0), (1, w1), (3, w3)):
            at = pl.multiple_of(lax.rem(x + r, N) * width, width)
            wide[:, pl.ds(at, width)] = piece[...]
        at = pl.multiple_of(lax.rem(x + 2, N) * width, width)
        wide[:, pl.ds(at, width // 2)] = w2a[...]
        wide[:, pl.ds(pl.multiple_of(at + width // 2, width // 2), width // 2)] = w2b[...]

    def fill(source):
        for r in range(N):
            at = pl.multiple_of(lax.rem(y + r, N) * width, width)
            rows[:, pl.ds(at, width)] = source[r]

    @pl.when(index[step] == 1)
    def _():
        fill(mine)

    @pl.when(index[step] == 0)
    def _():
        fill(other)

    result = lax.dot_general(
        rows[...], wide[...], CONTRACT_LAST, preferred_element_type=jnp.float32
    ).astype(jnp.bfloat16)
    half = result.shape[0] // 2

    @pl.when(step == 0)
    def _():
        outs[0][...] = result[:half]
        outs[1][...] = result[half:]

    @pl.when(step == 1)
    def _():
        outs[2][...] = result[:half]
        outs[3][...] = result[half:]


def products(even, index, mine, other, pieces):
    columns, width = pieces[0].shape
    tokens = mine.shape[1]
    shape = (tokens // 2, columns)

    def kernel(*refs):
        product_kernel(even, *refs)

    return pl.pallas_call(
        kernel,
        grid_spec=pltpu.PrefetchScalarGridSpec(
            num_scalar_prefetch=1,
            grid=(2,),
            in_specs=[whole(a) for a in (mine, other) + pieces],
            out_specs=[pl.BlockSpec(shape, lambda i, ix: (0, 0))] * 4,
            scratch_shapes=[
                pltpu.VMEM((columns, N * width), jnp.bfloat16),
                pltpu.VMEM((tokens, N * width), jnp.bfloat16),
            ],
        ),
        out_shape=[jax.ShapeDtypeStruct(shape, jnp.bfloat16)] * 4,
        compiler_params=pltpu.CompilerParams(vmem_limit_bytes=VMEM),
        cost_estimate=pl.CostEstimate(
            flops=4 * tokens * N * width * columns,
            bytes_accessed=2 * (4 * tokens * N * width + columns * N * width),
            transcendentals=0,
        ),
    )(index, mine, other, *pieces)


def finish_kernel(slots, summed, a_in, *refs):
    out = refs[-1]
    rank = a_in.shape[1]
    low = lax.dot_general(
        summed[:, :rank], a_in[0], (((1,), (0,)), ((), ())), preferred_element_type=jnp.float32
    )
    upper = pl.program_id(0) < 2
    start = 0
    for k in range(len(CHUNKS)):
        lows, highs = refs[k * 6 : k * 6 + 3], refs[k * 6 + 3 : k * 6 + 6]
        columns = lows[0].shape[1]

        def write(parts, start=start, columns=columns):
            total = adapter_scale * low[:, start : start + columns]
            for part in parts:
                total = total + part[...].astype(jnp.float32)
            out[:, start : start + columns] = total.astype(out.dtype)

        @pl.when(upper)
        def _():
            write(lows)

        @pl.when(jnp.logical_not(upper))
        def _():
            write(highs)

        start += columns


def finish(slots, summed, adapter_in, parts):
    tokens, twice = summed.shape
    blocks = slots.shape[0]
    rows = tokens // blocks
    rank, units = adapter_in.shape[1:]
    low = lambda a: pl.BlockSpec((rows, a.shape[1]), lambda i, s: (jnp.minimum(i, 1), 0))
    high = lambda a: pl.BlockSpec((rows, a.shape[1]), lambda i, s: (jnp.maximum(i - 2, 0), 0))
    specs = [low(a) if n % 6 < 3 else high(a) for n, a in enumerate(parts)]
    return pl.pallas_call(
        finish_kernel,
        grid_spec=pltpu.PrefetchScalarGridSpec(
            num_scalar_prefetch=1,
            grid=(blocks,),
            in_specs=[
                pl.BlockSpec((rows, twice), lambda i, s: (i, 0)),
                pl.BlockSpec((1, rank, units), lambda i, s: (s[i], 0, 0)),
            ]
            + specs,
            out_specs=pl.BlockSpec((rows, units), lambda i, s: (i, 0)),
        ),
        out_shape=jax.ShapeDtypeStruct((tokens, units), jnp.bfloat16),
        compiler_params=pltpu.CompilerParams(vmem_limit_bytes=VMEM),
    )(slots, summed, adapter_in, *parts)


def scatter_sum(far, right, left, own, axis):
    via_low = take_from(far[0], axis, -1)
    via_high = take_from(far[1], axis, 1)
    right_high = take_from(right[1], axis, -1)
    left_low = take_from(left[0], axis, 1)
    right_low = take_from(right[0] + via_low, axis, -1)
    left_high = take_from(left[1] + via_high, axis, 1)
    return (own[0], left_low, right_low), (own[1], right_high, left_high)


def body(hidden, cotangent, down_weight, adapter_in, adapter_out, adapter_ids, adapter_slot):
    tokens, units = hidden.shape
    x, y = lax.axis_index("x"), lax.axis_index("y")
    core, z = lax.axis_index("c"), lax.axis_index("z")
    slots = adapter_slot[adapter_ids[:, 0]]

    width = cotangent.shape[1] // 2
    turned = []
    for k in range(2):
        at = lax.rem(z + k, 2) * width
        piece = lax.dynamic_slice_in_dim(cotangent, at, width, axis=1)
        pairs = [
            (c * N + d, (d // 2) * N + 2 * c + (d + k) % 2) for c in range(2) for d in range(N)
        ]
        turned.append(lax.ppermute(piece, ("c", "z"), pairs))

    weights = []
    start = 0
    for columns in CHUNKS:
        piece = lax.slice_in_dim(down_weight, start, start + columns, axis=0)
        weights.append((piece,) + gather_ring(piece, "x", 1))
        start += columns

    summed = sum_over_dp(rank_sums(slots, cotangent, hidden, adapter_out, adapter_in))

    flows = []
    for piece in turned:
        after, before, far_low, far_high = gather_ring(piece, "y", 0)
        mine = jnp.stack([piece, after, jnp.concatenate([far_low, far_high], axis=0), before])
        flows.append((mine, other_core(mine)))

    def ours(step):
        return (lax.rem(z + step, N) // 2 == core).astype(jnp.int32)

    index = [
        jnp.stack([ours(a), ours(b), x, y]).astype(jnp.int32) for a, b in ((2, 0), (1, 3))
    ]
    parts = []
    for pieces in weights:
        far_low, far_high, own_low, own_high = products(True, index[0], *flows[0], pieces)
        right_low, right_high, left_low, left_high = products(False, index[1], *flows[1], pieces)
        lows, highs = scatter_sum(
            (far_low, far_high), (right_low, right_high), (left_low, left_high), (own_low, own_high), "z"
        )
        parts.extend(lows + highs)
    hidden_gradient = finish(slots, summed, adapter_in, parts)

    terms = gradient_terms(
        slots, x, z, summed, cotangent, hidden, adapter_scale / math.sqrt(tokens)
    )
    half = terms[0].shape[0]
    own = terms[6]
    lows, highs = scatter_sum(terms[0:2], terms[2:4], terms[4:6], (own[:half], own[half:]), "x")
    rank = half // 2

    def added(parts, at):
        return sum(p[at : at + rank].astype(jnp.float32) for p in parts)

    across = take_from(added(lows, 0).astype(jnp.bfloat16), "z", 2)
    before = take_from(added(lows, rank).astype(jnp.bfloat16), "z", -1)
    after = take_from(added(highs, 0).astype(jnp.bfloat16), "z", 1)
    total = added(highs, rank)
    for part in (across, before, after):
        total = total + part.astype(jnp.float32)
    grads = total.astype(jnp.bfloat16)[None]
    split = cotangent.shape[1]
    return hidden_gradient, grads[:, :, split:], grads[:, :, :split]


def solution(mesh):
    fine = Mesh(mesh.devices.reshape(N, 2, N, N), ("y", "c", "x", "z"))
    dp, fsdp = ("y", "c"), ("x", "z")
    placed = (
        P(fsdp, dp),
        P(fsdp, dp),
        P(dp, fsdp),
        P(None, None, dp),
        P(None, None, dp),
        P(fsdp, None),
        P(),
    )
    return jax.shard_map(
        body,
        mesh=fine,
        in_specs=placed,
        out_specs=(P(fsdp, dp), P(fsdp, None, dp), P(fsdp, None, dp)),
        check_vma=False,
    )
```

```python
import math

import jax
import jax.numpy as jnp
from jax import lax
from jax.experimental import pallas as pl
from jax.experimental.pallas import tpu as pltpu
from jax.sharding import Mesh, PartitionSpec as P

adapter_scale = 2.0
N = 4
MIB = 1024 * 1024
NN = (((1,), (0,)), ((), ()))
NT = (((1,), (1,)), ((), ()))
TN = (((0,), (0,)), ((), ()))


def take_from(array, axis, step):
    return lax.ppermute(array, axis, [((i + step) % N, i) for i in range(N)])


def other_core(array):
    return lax.ppermute(array, "c", [(0, 1), (1, 0)])


def sum_over_dp(array):
    array = array + other_core(array)
    array = array + lax.ppermute(array, "y", [(0, 1), (1, 0), (2, 3), (3, 2)])
    return array + lax.ppermute(array, "y", [(0, 3), (3, 0), (1, 2), (2, 1)])


def scatter_ring(far, right, left, own, axis, way):
    via = take_from(far, axis, -way)
    if way > 0:
        left = take_from(left, axis, 1)
        right = take_from(right + via, axis, -1)
    else:
        right = take_from(right, axis, -1)
        left = take_from(left + via, axis, 1)
    return [own, left, right]


def whole(array):
    return pl.BlockSpec(array.shape, lambda i, ix: (0,) * array.ndim)


def call(kernel, grid, operands, in_specs, out_specs, out_shape, scratch, mib):
    return pl.pallas_call(
        kernel,
        grid_spec=pltpu.PrefetchScalarGridSpec(
            num_scalar_prefetch=1,
            grid=grid,
            in_specs=in_specs,
            out_specs=out_specs,
            scratch_shapes=scratch,
        ),
        out_shape=out_shape,
        compiler_params=pltpu.CompilerParams(vmem_limit_bytes=mib * MIB),
        cost_estimate=pl.CostEstimate(flops=1000000, bytes_accessed=1000000, transcendentals=0),
    )(*operands)


def rank_sums(slots, cotangent, hidden, adapter_out, adapter_in):
    tokens, width = cotangent.shape
    units = hidden.shape[0]
    rank = adapter_in.shape[1]
    blocks = slots.shape[0]
    rows = tokens // blocks

    def kernel(slots, cotangent, hidden, a_out, a_in, out, cot, hid, outs, ins, sems):
        copies = [
            pltpu.make_async_copy(cotangent, cot, sems.at[0]),
            pltpu.make_async_copy(hidden, hid, sems.at[1]),
        ]
        for b in range(blocks):
            copies.append(pltpu.make_async_copy(a_out.at[slots[b]], outs.at[b], sems.at[2 + b]))
        for b in range(blocks):
            copies.append(
                pltpu.make_async_copy(a_in.at[slots[b]], ins.at[b], sems.at[2 + blocks + b])
            )
        for copy in copies:
            copy.start()
        for copy in copies:
            copy.wait()
        for b in range(blocks):
            at = slice(b * rows, (b + 1) * rows)
            out[:rank, at] = lax.dot_general(
                outs[b], cot[at, :], NT, preferred_element_type=jnp.float32
            ).astype(out.dtype)
            out[rank:, at] = lax.dot_general(
                ins[b], hid[:, at], NN, preferred_element_type=jnp.float32
            ).astype(out.dtype)

    far = pl.BlockSpec(memory_space=pltpu.HBM)
    return call(
        kernel,
        (1,),
        (slots, cotangent, hidden, adapter_out, adapter_in),
        [far] * 4,
        pl.BlockSpec(memory_space=pltpu.VMEM),
        jax.ShapeDtypeStruct((2 * rank, tokens), jnp.bfloat16),
        [
            pltpu.VMEM((tokens, width), jnp.bfloat16),
            pltpu.VMEM((units, tokens), jnp.bfloat16),
            pltpu.VMEM((blocks, rank, width), jnp.bfloat16),
            pltpu.VMEM((blocks, rank, units), jnp.bfloat16),
            pltpu.SemaphoreType.DMA((2 + 2 * blocks,)),
        ],
        8,
    )


def terms_kernel(multiplier, index, summed, cotangent, hidden, *refs):
    outs, products = refs[:8], refs[8]
    blocks = products.shape[0]
    rows = cotangent.shape[0] // blocks
    width = cotangent.shape[1]
    units = hidden.shape[0]
    rank = summed.shape[0] // 2
    for b in range(blocks):
        at = slice(b * rows, (b + 1) * rows)
        products[b, :, :width] = lax.dot_general(
            summed[rank:, at], cotangent[at, :], NN, preferred_element_type=jnp.float32
        )
        products[b, :, width : width + units] = lax.dot_general(
            summed[:rank, at], hidden[:, at], NT, preferred_element_type=jnp.float32
        )
        products[b, :, width + units :] = jnp.zeros(
            (rank, products.shape[2] - width - units), jnp.float32
        )
    x, z = index[blocks], index[blocks + 1]
    for place, s in enumerate((2, 1, 3, 0)):
        for part, t in enumerate((2, 1, 3, 0)):
            slot = lax.rem(x + t, N) * N + lax.rem(z + s, N)
            total = jnp.zeros(products.shape[1:], jnp.float32)
            for b in range(blocks):
                weight = jnp.where(index[b] == slot, jnp.float32(multiplier), jnp.float32(0))
                total = total + weight * products[b]
            ref = outs[place * 2 + part // 2]
            row = part % 2 * rank
            ref[row : row + rank, :] = total.astype(ref.dtype)


def gradient_terms(index, summed, cotangent, hidden, multiplier):
    blocks = index.shape[0] - 2
    wide = cotangent.shape[1] + hidden.shape[0]
    wide = wide + -wide % 128
    rank = summed.shape[0] // 2
    shape = (2 * rank, wide)

    def kernel(*refs):
        terms_kernel(multiplier, *refs)

    return call(
        kernel,
        (1,),
        (index, summed, cotangent, hidden),
        [whole(a) for a in (summed, cotangent, hidden)],
        [pl.BlockSpec(memory_space=pltpu.VMEM)] * 8,
        [jax.ShapeDtypeStruct(shape, jnp.bfloat16)] * 8,
        [pltpu.VMEM((blocks, rank, wide), jnp.float32)],
        20,
    )


def added(refs, at):
    total = refs[0][at, :].astype(jnp.float32)
    for ref in refs[1:]:
        total = total + ref[at, :].astype(jnp.float32)
    return total


def middle_kernel(*refs):
    outs = refs[6:]
    rank = outs[0].shape[0]
    for n, out in enumerate(outs):
        at = slice(n % 2 * rank, (n % 2 + 1) * rank)
        out[...] = added(refs[n // 2 * 3 : n // 2 * 3 + 3], at).astype(out.dtype)


def middle_sums(lows, highs):
    rows, wide = lows[0].shape
    shape = (rows // 2, wide)
    kinds = [jnp.bfloat16] * 3 + [jnp.float32]
    return pl.pallas_call(
        middle_kernel,
        out_shape=[jax.ShapeDtypeStruct(shape, kind) for kind in kinds],
        compiler_params=pltpu.CompilerParams(vmem_limit_bytes=10 * MIB),
        cost_estimate=pl.CostEstimate(flops=1000000, bytes_accessed=1000000, transcendentals=0),
    )(*lows, *highs)


def last_kernel(own, across, before, after, out_in, out_out):
    split, units = out_out.shape[2], out_in.shape[2]
    total = added((own, across, before, after), slice(None))
    out_out[0] = total[:, :split].astype(out_out.dtype)
    out_in[0] = total[:, split : split + units].astype(out_in.dtype)


def last_sum(parts, units, width):
    rank = parts[0].shape[0]
    return pl.pallas_call(
        last_kernel,
        out_shape=[jax.ShapeDtypeStruct((1, rank, n), jnp.bfloat16) for n in (units, width)],
        compiler_params=pltpu.CompilerParams(vmem_limit_bytes=6 * MIB),
        cost_estimate=pl.CostEstimate(flops=1000000, bytes_accessed=1000000, transcendentals=0),
    )(*parts)


def products(index, gathered, weights, steps):
    rows, width = weights[0].shape
    tokens = gathered.shape[3]

    def kernel(index, gathered, *refs):
        pieces, outs, held, sides, sems = refs[:N], refs[N : N + 2], refs[-3], refs[-2], refs[-1]
        copies = {}
        for n, step in enumerate(steps):
            for r in range(N):
                copies[n, r] = pltpu.make_async_copy(
                    gathered.at[lax.rem(index[2] + r, N), index[n], step % 2],
                    sides.at[n, r],
                    sems.at[n, r],
                )
                copies[n, r].start()
                if n == 0:
                    copies[2, r] = pltpu.make_async_copy(pieces[r], held.at[r], sems.at[2, r])
                    copies[2, r].start()
        for n in range(2):
            total = None
            for r in range(N):
                if n == 0:
                    copies[2, r].wait()
                copies[n, r].wait()
                part = lax.dot_general(
                    held[r], sides[n, r], NT, preferred_element_type=jnp.float32
                )
                total = part if total is None else total + part
            outs[n][...] = total.astype(jnp.bfloat16)

    shape = (rows, tokens)
    return call(
        kernel,
        (1,),
        [index, gathered, *weights],
        [pl.BlockSpec(memory_space=pltpu.HBM)] + [pl.BlockSpec(memory_space=pl.ANY)] * N,
        [pl.BlockSpec(memory_space=pltpu.VMEM)] * 2,
        [jax.ShapeDtypeStruct(shape, jnp.bfloat16)] * 2,
        [
            pltpu.VMEM((N, rows, width), jnp.bfloat16),
            pltpu.VMEM((2, N, tokens, width), jnp.bfloat16),
            pltpu.SemaphoreType.DMA((3, N)),
        ],
        20,
    )


def finish_kernel(slots, summed, a_in, *refs):
    out = refs[-1]
    rank = a_in.shape[1]
    low = adapter_scale * lax.dot_general(
        a_in[0], summed[:rank, :], TN, preferred_element_type=jnp.float32
    )
    start = 0
    for k in range(0, len(refs) - 1, 3):
        rows = refs[k].shape[0]
        total = low[start : start + rows] + added(refs[k : k + 3], slice(None))
        out[start : start + rows, :] = total.astype(out.dtype)
        start += rows


def finish(slots, summed, adapter_in, parts):
    twice, tokens = summed.shape
    blocks = slots.shape[0]
    rows = tokens // blocks
    rank, units = adapter_in.shape[1:]
    return call(
        finish_kernel,
        (blocks,),
        [slots, summed, adapter_in] + parts,
        [
            pl.BlockSpec((twice, rows), lambda i, s: (0, i)),
            pl.BlockSpec((1, rank, units), lambda i, s: (s[i], 0, 0)),
        ]
        + [pl.BlockSpec((p.shape[0], rows), lambda i, s: (0, i)) for p in parts],
        pl.BlockSpec((units, rows), lambda i, s: (0, i)),
        jax.ShapeDtypeStruct((units, tokens), jnp.bfloat16),
        [],
        10,
    )


def body(hidden, cotangent, down_weight, adapter_in, adapter_out, adapter_ids, adapter_slot):
    hidden = hidden.T
    units, tokens = hidden.shape
    x = lax.axis_index("x")
    z = lax.axis_index("z")
    slots = adapter_slot[adapter_ids[:, 0]]

    width = cotangent.shape[1] // 2
    turned = []
    for k in range(2):
        at = lax.rem(z + k, 2) * width
        piece = lax.dynamic_slice_in_dim(cotangent, at, width, axis=1)
        pairs = [
            (c * N + d, (d // 2) * N + 2 * c + (d + k) % 2) for c in range(2) for d in range(N)
        ]
        turned.append(lax.ppermute(piece, ("c", "z"), pairs))
    first = (units // 2 + 15) // 16 * 16
    own = [down_weight[:first], down_weight[first:]]
    after = [take_from(p, "x", 1) for p in own]
    before = [take_from(p, "x", -1) for p in own]

    ranks = rank_sums(slots, cotangent, hidden, adapter_out, adapter_in)
    turned[0], turned[1], after[0], before[0], ranks = lax.optimization_barrier(
        (turned[0], turned[1], after[0], before[0], ranks)
    )
    gathered = lax.all_gather(jnp.stack(turned), ("y", "c"))
    gathered = gathered.reshape(N, 2, 2, tokens, width)
    summed = sum_over_dp(ranks)
    index = jnp.concatenate([slots, jnp.stack([x, z]).astype(jnp.int32)])
    terms = gradient_terms(index, summed, cotangent, hidden, adapter_scale / math.sqrt(tokens))
    after[0], after[1], before[1], *terms = lax.optimization_barrier(
        (after[0], after[1], before[1], *terms)
    )
    fars = [take_from(after[0], "x", 1), take_from(before[1], "x", -1)]

    def make(chunk, *steps):
        index = jnp.stack([lax.rem(z + s, N) // 2 for s in steps] + [x]).astype(jnp.int32)
        weights = (own[chunk], after[chunk], fars[chunk], before[chunk])
        return products(index, gathered, weights, steps)

    far0, left0 = make(0, 2, 3)
    far1, right1 = make(1, 2, 1)
    right0, own0 = make(0, 1, 0)
    left1, own1 = make(1, 3, 0)
    parts = scatter_ring(far0, right0, left0, own0, "z", 1)
    parts += scatter_ring(far1, right1, left1, own1, "z", -1)
    hidden_gradient = finish(slots, summed, adapter_in, parts)

    lows = scatter_ring(*terms[0::2], "z", 1)
    highs = scatter_ring(*terms[1::2], "z", -1)
    across, before, after, own = middle_sums(lows, highs)
    others = [take_from(p, "x", s) for p, s in ((across, 2), (before, -1), (after, 1))]
    grad_in, grad_out = last_sum([own] + others, units, cotangent.shape[1])
    return hidden_gradient.T, grad_in, grad_out


def solution(mesh):
    fine = Mesh(mesh.devices.reshape(N, 2, N, N), ("y", "c", "x", "z"))
    dp, fsdp = ("y", "c"), ("x", "z")
    placed = (
        P(fsdp, dp),
        P(fsdp, dp),
        P(dp, fsdp),
        P(None, None, dp),
        P(None, None, dp),
        P(fsdp, None),
        P(),
    )
    return jax.shard_map(
        body,
        mesh=fine,
        in_specs=placed,
        out_specs=(P(fsdp, dp), P(fsdp, None, dp), P(fsdp, None, dp)),
        check_vma=False,
    )
```

```python
import math

import jax
import jax.numpy as jnp
from jax import lax
from jax.experimental import pallas as pl
from jax.experimental.pallas import tpu as pltpu
from jax.sharding import Mesh, PartitionSpec as P

adapter_scale = 2.0
N = 4
MIB = 1024 * 1024
BIG = 52
NN = (((1,), (0,)), ((), ()))
NT = (((1,), (1,)), ((), ()))
TN = (((0,), (0,)), ((), ()))


def take_from(array, axis, step):
    return lax.ppermute(array, axis, [((i + step) % N, i) for i in range(N)])


def other_core(array):
    return lax.ppermute(array, "c", [(0, 1), (1, 0)])


def sum_over_dp(array):
    array = array + other_core(array)
    array = array + lax.ppermute(array, "y", [(0, 1), (1, 0), (2, 3), (3, 2)])
    return array + lax.ppermute(array, "y", [(0, 3), (3, 0), (1, 2), (2, 1)])


def scatter_ring(far, right, left, own, axis, way):
    via = take_from(far, axis, -way)
    if way > 0:
        left = take_from(left, axis, 1)
        right = take_from(right + via, axis, -1)
    else:
        right = take_from(right, axis, -1)
        left = take_from(left + via, axis, 1)
    return [own, left, right]


def whole(array):
    return pl.BlockSpec(array.shape, lambda i, ix: (0,) * array.ndim)


def call(kernel, grid, operands, in_specs, out_specs, out_shape, scratch, mib):
    return pl.pallas_call(
        kernel,
        grid_spec=pltpu.PrefetchScalarGridSpec(
            num_scalar_prefetch=1,
            grid=grid,
            in_specs=in_specs,
            out_specs=out_specs,
            scratch_shapes=scratch,
        ),
        out_shape=out_shape,
        compiler_params=pltpu.CompilerParams(vmem_limit_bytes=mib * MIB),
        cost_estimate=pl.CostEstimate(flops=1000000, bytes_accessed=1000000, transcendentals=0),
    )(*operands)


def rank_sums(slots, cotangent, hidden, adapter_out, adapter_in):
    tokens, width = cotangent.shape
    units = hidden.shape[0]
    rank = adapter_in.shape[1]
    blocks = slots.shape[0]
    rows = tokens // blocks

    def kernel(slots, cotangent, hidden, a_out, a_in, out, cot, hid, outs, ins, sems):
        copies = [
            pltpu.make_async_copy(cotangent, cot, sems.at[0]),
            pltpu.make_async_copy(hidden, hid, sems.at[1]),
        ]
        for b in range(blocks):
            copies.append(pltpu.make_async_copy(a_out.at[slots[b]], outs.at[b], sems.at[2 + b]))
        for b in range(blocks):
            copies.append(
                pltpu.make_async_copy(a_in.at[slots[b]], ins.at[b], sems.at[2 + blocks + b])
            )
        for copy in copies:
            copy.start()
        for copy in copies:
            copy.wait()
        for b in range(blocks):
            at = slice(b * rows, (b + 1) * rows)
            out[:rank, at] = lax.dot_general(
                outs[b], cot[at, :], NT, preferred_element_type=jnp.float32
            ).astype(out.dtype)
            out[rank:, at] = lax.dot_general(
                ins[b], hid[:, at], NN, preferred_element_type=jnp.float32
            ).astype(out.dtype)

    far = pl.BlockSpec(memory_space=pltpu.HBM)
    return call(
        kernel,
        (1,),
        (slots, cotangent, hidden, adapter_out, adapter_in),
        [far] * 4,
        pl.BlockSpec(memory_space=pltpu.VMEM),
        jax.ShapeDtypeStruct((2 * rank, tokens), jnp.bfloat16),
        [
            pltpu.VMEM((tokens, width), jnp.bfloat16),
            pltpu.VMEM((units, tokens), jnp.bfloat16),
            pltpu.VMEM((blocks, rank, width), jnp.bfloat16),
            pltpu.VMEM((blocks, rank, units), jnp.bfloat16),
            pltpu.SemaphoreType.DMA((2 + 2 * blocks,)),
        ],
        BIG,
    )


def gradient_terms(index, summed, cotangent, hidden, multiplier):
    blocks = index.shape[0] - 1
    tokens, width = cotangent.shape
    rows = tokens // blocks
    units = hidden.shape[0]
    wide = width + units
    wide = wide + -wide % 128
    rank = summed.shape[0] // 2
    shape = (N, N * rank, wide)

    def kernel(index, summed, cotangent, hidden, out, products, staged, sems):
        for b in range(blocks):
            at = slice(b * rows, (b + 1) * rows)
            products[b, :, :width] = lax.dot_general(
                summed[rank:, at], cotangent[at, :], NN, preferred_element_type=jnp.float32
            )
            products[b, :, width : width + units] = lax.dot_general(
                summed[:rank, at], hidden[:, at], NT, preferred_element_type=jnp.float32
            )
            products[b, :, width + units :] = jnp.zeros((rank, wide - width - units), jnp.float32)
        x = index[blocks]
        copies = []
        for s in range(N):
            for t in range(N):
                slot = lax.rem(x + t, N) * N + s
                total = jnp.zeros((rank, wide), jnp.float32)
                for b in range(blocks):
                    weight = jnp.where(index[b] == slot, jnp.float32(multiplier), jnp.float32(0))
                    total = total + weight * products[b]
                staged[s, t * rank : (t + 1) * rank, :] = total.astype(staged.dtype)
            copies.append(pltpu.make_async_copy(staged.at[s], out.at[s], sems.at[s]))
            copies[s].start()
        for copy in copies:
            copy.wait()

    return call(
        kernel,
        (1,),
        (index, summed, cotangent, hidden),
        [whole(a) for a in (summed, cotangent, hidden)],
        pl.BlockSpec(memory_space=pl.ANY),
        jax.ShapeDtypeStruct(shape, jnp.bfloat16),
        [
            pltpu.VMEM((blocks, rank, wide), jnp.float32),
            pltpu.VMEM(shape, jnp.bfloat16),
            pltpu.SemaphoreType.DMA((N,)),
        ],
        BIG,
    )


def second_hop(sums, axis):
    rank = sums.shape[0] // N
    parts = [sums[t * rank : (t + 1) * rank] for t in range(N)]
    return [parts[0]] + [take_from(parts[t], axis, -t) for t in range(1, N)]


def added(refs, at):
    total = refs[0][at, :].astype(jnp.float32)
    for ref in refs[1:]:
        total = total + ref[at, :].astype(jnp.float32)
    return total


def last_kernel(own, across, before, after, out_in, out_out):
    split, units = out_out.shape[2], out_in.shape[2]
    total = added((own, across, before, after), slice(None))
    out_out[0] = total[:, :split].astype(out_out.dtype)
    out_in[0] = total[:, split : split + units].astype(out_in.dtype)


def last_sum(parts, units, width):
    rank = parts[0].shape[0]
    return pl.pallas_call(
        last_kernel,
        out_shape=[jax.ShapeDtypeStruct((1, rank, n), jnp.bfloat16) for n in (units, width)],
        compiler_params=pltpu.CompilerParams(vmem_limit_bytes=6 * MIB),
        cost_estimate=pl.CostEstimate(flops=1000000, bytes_accessed=1000000, transcendentals=0),
    )(*parts)


def packed(pieces):
    rows, width = pieces[0].shape

    def kernel(*refs):
        for n, ref in enumerate(refs[:-1]):
            refs[-1][n] = ref[...]

    return pl.pallas_call(
        kernel,
        grid=(2,),
        in_specs=[pl.BlockSpec((rows // 2, width), lambda i: (i, 0))] * len(pieces),
        out_specs=pl.BlockSpec((len(pieces), rows // 2, width), lambda i: (0, i, 0)),
        out_shape=jax.ShapeDtypeStruct((len(pieces), rows, width), pieces[0].dtype),
        compiler_params=pltpu.CompilerParams(vmem_limit_bytes=BIG * MIB),
        cost_estimate=pl.CostEstimate(flops=1000000, bytes_accessed=1000000, transcendentals=0),
    )(*pieces)


def products(index, gathered, weights, steps):
    rows, width = weights[0].shape
    tokens = gathered.shape[3]

    def kernel(index, gathered, *refs):
        pieces, outs, held, sides, sems = refs[:N], refs[N : N + 2], refs[-3], refs[-2], refs[-1]
        copies = {}
        for n, step in enumerate(steps):
            for r in range(N):
                copies[n, r] = pltpu.make_async_copy(
                    gathered.at[lax.rem(index[2] + r, N), index[n], step % 2],
                    sides.at[n, r],
                    sems.at[n, r],
                )
                copies[n, r].start()
                if n == 0:
                    copies[2, r] = pltpu.make_async_copy(pieces[r], held.at[r], sems.at[2, r])
                    copies[2, r].start()
        for n in range(2):
            total = None
            for r in range(N):
                if n == 0:
                    copies[2, r].wait()
                copies[n, r].wait()
                part = lax.dot_general(
                    held[r], sides[n, r], NT, preferred_element_type=jnp.float32
                )
                total = part if total is None else total + part
            outs[n][...] = total.astype(jnp.bfloat16)

    shape = (rows, tokens)
    return call(
        kernel,
        (1,),
        [index, gathered, *weights],
        [pl.BlockSpec(memory_space=pltpu.HBM)] + [pl.BlockSpec(memory_space=pl.ANY)] * N,
        [pl.BlockSpec(memory_space=pltpu.VMEM)] * 2,
        [jax.ShapeDtypeStruct(shape, jnp.bfloat16)] * 2,
        [
            pltpu.VMEM((N, rows, width), jnp.bfloat16),
            pltpu.VMEM((2, N, tokens, width), jnp.bfloat16),
            pltpu.SemaphoreType.DMA((3, N)),
        ],
        BIG,
    )


def finish_kernel(slots, summed, a_in, *refs):
    out = refs[-1]
    rank = a_in.shape[1]
    low = adapter_scale * lax.dot_general(
        a_in[0], summed[:rank, :], TN, preferred_element_type=jnp.float32
    )
    start = 0
    for k in range(0, len(refs) - 1, 3):
        rows = refs[k].shape[0]
        total = low[start : start + rows] + added(refs[k : k + 3], slice(None))
        out[start : start + rows, :] = total.astype(out.dtype)
        start += rows


def finish(slots, summed, adapter_in, parts):
    twice, tokens = summed.shape
    blocks = slots.shape[0]
    rows = tokens // blocks
    rank, units = adapter_in.shape[1:]
    return call(
        finish_kernel,
        (blocks,),
        [slots, summed, adapter_in] + parts,
        [
            pl.BlockSpec((twice, rows), lambda i, s: (0, i)),
            pl.BlockSpec((1, rank, units), lambda i, s: (s[i], 0, 0)),
        ]
        + [pl.BlockSpec((p.shape[0], rows), lambda i, s: (0, i)) for p in parts],
        pl.BlockSpec((units, rows), lambda i, s: (0, i)),
        jax.ShapeDtypeStruct((units, tokens), jnp.bfloat16),
        [],
        BIG,
    )


def body(hidden, cotangent, down_weight, adapter_in, adapter_out, adapter_ids, adapter_slot):
    hidden = hidden.T
    units, tokens = hidden.shape
    x = lax.axis_index("x")
    z = lax.axis_index("z")
    slots = adapter_slot[adapter_ids[:, 0]]

    width = cotangent.shape[1] // 2
    turned = []
    for k in range(2):
        at = lax.rem(z + k, 2) * width
        piece = lax.dynamic_slice_in_dim(cotangent, at, width, axis=1)
        pairs = [
            (c * N + d, (d // 2) * N + 2 * c + (d + k) % 2) for c in range(2) for d in range(N)
        ]
        turned.append(lax.ppermute(piece, ("c", "z"), pairs))
    first = (units // 2 + 15) // 16 * 16
    own = [down_weight[:first], down_weight[first:]]
    after, before = [take_from(own[0], "x", 1)], [take_from(own[0], "x", -1)]

    barrier = lax.optimization_barrier
    summed = sum_over_dp(rank_sums(slots, cotangent, hidden, adapter_out, adapter_in))
    *turned, after[0], before[0], summed, own[1] = barrier(
        (*turned, after[0], before[0], summed, own[1])
    )
    gathered = lax.all_gather(packed(turned), ("y", "c")).reshape(N, 2, 2, tokens, width)
    after.append(take_from(own[1], "x", 1))
    before.append(take_from(own[1], "x", -1))
    index = jnp.concatenate([slots, x[None].astype(jnp.int32)])
    terms = gradient_terms(index, summed, cotangent, hidden, adapter_scale / math.sqrt(tokens))
    sums = lax.psum_scatter(terms, "z", scatter_dimension=0)
    after[0], after[1], before[1], terms = barrier((after[0], after[1], before[1], terms))
    fars = [take_from(after[0], "x", 1), take_from(before[1], "x", -1)]

    def make(chunk, *steps):
        index = jnp.stack([lax.rem(z + s, N) // 2 for s in steps] + [x]).astype(jnp.int32)
        weights = (own[chunk], after[chunk], fars[chunk], before[chunk])
        return products(index, gathered, weights, steps)

    far0, left0 = make(0, 2, 3)
    far1, right1 = make(1, 2, 1)
    right0, own0 = make(0, 1, 0)
    left1, own1 = make(1, 3, 0)
    parts = scatter_ring(far0, right0, left0, own0, "z", 1)
    parts += scatter_ring(far1, right1, left1, own1, "z", -1)
    hidden_gradient = finish(slots, summed, adapter_in, parts)

    grad_in, grad_out = last_sum(second_hop(sums, "x"), units, cotangent.shape[1])
    return hidden_gradient.T, grad_in, grad_out


def solution(mesh):
    fine = Mesh(mesh.devices.reshape(N, 2, N, N), ("y", "c", "x", "z"))
    dp, fsdp = ("y", "c"), ("x", "z")
    placed = (
        P(fsdp, dp),
        P(fsdp, dp),
        P(dp, fsdp),
        P(None, None, dp),
        P(None, None, dp),
        P(fsdp, None),
        P(),
    )
    return jax.shard_map(
        body,
        mesh=fine,
        in_specs=placed,
        out_specs=(P(fsdp, dp), P(fsdp, None, dp), P(fsdp, None, dp)),
        check_vma=False,
    )
```

```python
import math

import jax
import jax.numpy as jnp
from jax import lax
from jax.experimental import pallas as pl
from jax.experimental.pallas import tpu as pltpu
from jax.sharding import Mesh, PartitionSpec as P

adapter_scale = 2.0
N = 4
MIB = 1024 * 1024
BIG = 52
NN = (((1,), (0,)), ((), ()))
NT = (((1,), (1,)), ((), ()))
TN = (((0,), (0,)), ((), ()))


def take_from(array, axis, step):
    return lax.ppermute(array, axis, [((i + step) % N, i) for i in range(N)])


def other_core(array):
    return lax.ppermute(array, "c", [(0, 1), (1, 0)])


def sum_over_dp(array):
    array = array + other_core(array)
    array = array + lax.ppermute(array, "y", [(0, 1), (1, 0), (2, 3), (3, 2)])
    return array + lax.ppermute(array, "y", [(0, 3), (3, 0), (1, 2), (2, 1)])


def scatter_ring(far, right, left, own, axis, way):
    via = take_from(far, axis, -way)
    if way > 0:
        left = take_from(left, axis, 1)
        right = take_from(right + via, axis, -1)
    else:
        right = take_from(right, axis, -1)
        left = take_from(left + via, axis, 1)
    return [own, left, right]


def whole(array):
    return pl.BlockSpec(array.shape, lambda i, ix: (0,) * array.ndim)


def call(kernel, grid, operands, in_specs, out_specs, out_shape, scratch, mib):
    return pl.pallas_call(
        kernel,
        grid_spec=pltpu.PrefetchScalarGridSpec(
            num_scalar_prefetch=1,
            grid=grid,
            in_specs=in_specs,
            out_specs=out_specs,
            scratch_shapes=scratch,
        ),
        out_shape=out_shape,
        compiler_params=pltpu.CompilerParams(vmem_limit_bytes=mib * MIB),
        cost_estimate=pl.CostEstimate(flops=1000000, bytes_accessed=1000000, transcendentals=0),
    )(*operands)


def rank_sums(slots, cotangent, hidden, adapter_out, adapter_in):
    tokens, width = cotangent.shape
    units = hidden.shape[0]
    rank = adapter_in.shape[1]
    blocks = slots.shape[0]
    rows = tokens // blocks

    def kernel(slots, cotangent, hidden, a_out, a_in, out, cot, hid, outs, ins, sems):
        copies = [
            pltpu.make_async_copy(cotangent, cot, sems.at[0]),
            pltpu.make_async_copy(hidden, hid, sems.at[1]),
        ]
        for b in range(blocks):
            copies.append(pltpu.make_async_copy(a_out.at[slots[b]], outs.at[b], sems.at[2 + b]))
        for b in range(blocks):
            copies.append(
                pltpu.make_async_copy(a_in.at[slots[b]], ins.at[b], sems.at[2 + blocks + b])
            )
        for copy in copies:
            copy.start()
        for copy in copies:
            copy.wait()
        for b in range(blocks):
            at = slice(b * rows, (b + 1) * rows)
            out[:rank, at] = lax.dot_general(
                outs[b], cot[at, :], NT, preferred_element_type=jnp.float32
            ).astype(out.dtype)
            out[rank:, at] = lax.dot_general(
                ins[b], hid[:, at], NN, preferred_element_type=jnp.float32
            ).astype(out.dtype)

    far = pl.BlockSpec(memory_space=pltpu.HBM)
    return call(
        kernel,
        (1,),
        (slots, cotangent, hidden, adapter_out, adapter_in),
        [far] * 4,
        pl.BlockSpec(memory_space=pltpu.VMEM),
        jax.ShapeDtypeStruct((2 * rank, tokens), jnp.bfloat16),
        [
            pltpu.VMEM((tokens, width), jnp.bfloat16),
            pltpu.VMEM((units, tokens), jnp.bfloat16),
            pltpu.VMEM((blocks, rank, width), jnp.bfloat16),
            pltpu.VMEM((blocks, rank, units), jnp.bfloat16),
            pltpu.SemaphoreType.DMA((2 + 2 * blocks,)),
        ],
        BIG,
    )


def gradient_terms(index, summed, cotangent, hidden, multiplier):
    blocks = index.shape[0] - 1
    tokens, width = cotangent.shape
    rows = tokens // blocks
    units = hidden.shape[0]
    wide = width + units
    wide = wide + -wide % 128
    rank = summed.shape[0] // 2
    shape = (N, N * rank, wide)

    def kernel(index, summed, cotangent, hidden, out, products, staged, sems):
        for b in range(blocks):
            at = slice(b * rows, (b + 1) * rows)
            products[b, :, :width] = lax.dot_general(
                summed[rank:, at], cotangent[at, :], NN, preferred_element_type=jnp.float32
            )
            products[b, :, width : width + units] = lax.dot_general(
                summed[:rank, at], hidden[:, at], NT, preferred_element_type=jnp.float32
            )
            products[b, :, width + units :] = jnp.zeros((rank, wide - width - units), jnp.float32)
        x = index[blocks]
        copies = []
        for s in range(N):
            for t in range(N):
                slot = lax.rem(x + t, N) * N + s
                total = jnp.zeros((rank, wide), jnp.float32)
                for b in range(blocks):
                    weight = jnp.where(index[b] == slot, jnp.float32(multiplier), jnp.float32(0))
                    total = total + weight * products[b]
                staged[s, t * rank : (t + 1) * rank, :] = total.astype(staged.dtype)
            copies.append(pltpu.make_async_copy(staged.at[s], out.at[s], sems.at[s]))
            copies[s].start()
        for copy in copies:
            copy.wait()

    return call(
        kernel,
        (1,),
        (index, summed, cotangent, hidden),
        [whole(a) for a in (summed, cotangent, hidden)],
        pl.BlockSpec(memory_space=pl.ANY),
        jax.ShapeDtypeStruct(shape, jnp.bfloat16),
        [
            pltpu.VMEM((blocks, rank, wide), jnp.float32),
            pltpu.VMEM(shape, jnp.bfloat16),
            pltpu.SemaphoreType.DMA((N,)),
        ],
        BIG,
    )


def second_hop(sums, axis):
    rank = sums.shape[0] // N
    parts = [sums[t * rank : (t + 1) * rank] for t in range(N)]
    return [parts[0]] + [take_from(parts[t], axis, -t) for t in range(1, N)]


def added(refs, at):
    total = refs[0][at, :].astype(jnp.float32)
    for ref in refs[1:]:
        total = total + ref[at, :].astype(jnp.float32)
    return total


def last_kernel(own, across, before, after, out_in, out_out):
    split, units = out_out.shape[2], out_in.shape[2]
    total = added((own, across, before, after), slice(None))
    out_out[0] = total[:, :split].astype(out_out.dtype)
    out_in[0] = total[:, split : split + units].astype(out_in.dtype)


def last_sum(parts, units, width):
    rank = parts[0].shape[0]
    return pl.pallas_call(
        last_kernel,
        out_shape=[jax.ShapeDtypeStruct((1, rank, n), jnp.bfloat16) for n in (units, width)],
        compiler_params=pltpu.CompilerParams(vmem_limit_bytes=6 * MIB),
        cost_estimate=pl.CostEstimate(flops=1000000, bytes_accessed=1000000, transcendentals=0),
    )(*parts)


def packed(pieces):
    rows, width = pieces[0].shape

    def kernel(*refs):
        for n, ref in enumerate(refs[:-1]):
            refs[-1][n] = ref[...]

    return pl.pallas_call(
        kernel,
        grid=(2,),
        in_specs=[pl.BlockSpec((rows // 2, width), lambda i: (i, 0))] * len(pieces),
        out_specs=pl.BlockSpec((len(pieces), rows // 2, width), lambda i: (0, i, 0)),
        out_shape=jax.ShapeDtypeStruct((len(pieces), rows, width), pieces[0].dtype),
        compiler_params=pltpu.CompilerParams(vmem_limit_bytes=BIG * MIB),
        cost_estimate=pl.CostEstimate(flops=1000000, bytes_accessed=1000000, transcendentals=0),
    )(*pieces)


def products(index, gathered, weights, steps):
    rows, width = weights[0].shape
    tokens = gathered.shape[3]

    def kernel(index, gathered, *refs):
        pieces, outs, held, sides, sems = refs[:N], refs[N : N + 2], refs[-3], refs[-2], refs[-1]
        copies = {}
        for n, step in enumerate(steps):
            for r in range(N):
                copies[n, r] = pltpu.make_async_copy(
                    gathered.at[lax.rem(index[2] + r, N), index[n], step % 2],
                    sides.at[n, r],
                    sems.at[n, r],
                )
                copies[n, r].start()
                if n == 0:
                    copies[2, r] = pltpu.make_async_copy(pieces[r], held.at[r], sems.at[2, r])
                    copies[2, r].start()
        for n in range(2):
            total = None
            for r in range(N):
                if n == 0:
                    copies[2, r].wait()
                copies[n, r].wait()
                part = lax.dot_general(
                    held[r], sides[n, r], NT, preferred_element_type=jnp.float32
                )
                total = part if total is None else total + part
            outs[n][...] = total.astype(jnp.bfloat16)

    shape = (rows, tokens)
    return call(
        kernel,
        (1,),
        [index, gathered, *weights],
        [pl.BlockSpec(memory_space=pltpu.HBM)] + [pl.BlockSpec(memory_space=pl.ANY)] * N,
        [pl.BlockSpec(memory_space=pltpu.VMEM)] * 2,
        [jax.ShapeDtypeStruct(shape, jnp.bfloat16)] * 2,
        [
            pltpu.VMEM((N, rows, width), jnp.bfloat16),
            pltpu.VMEM((2, N, tokens, width), jnp.bfloat16),
            pltpu.SemaphoreType.DMA((3, N)),
        ],
        BIG,
    )


def early_sums(slots, summed, adapter_in, parts):
    twice, tokens = summed.shape
    blocks = slots.shape[0]
    rows = tokens // blocks
    rank, units = adapter_in.shape[1:]
    flat = [p for chunk in parts for p in chunk]

    def kernel(slots, summed, a_in, *refs):
        low = adapter_scale * lax.dot_general(
            a_in[0], summed[:rank, :], TN, preferred_element_type=jnp.float32
        )
        start, at = 0, 0
        for chunk, out in zip(parts, refs[len(flat) :]):
            size = out.shape[0]
            total = low[start : start + size] + added(refs[at : at + len(chunk)], slice(None))
            out[...] = total.astype(out.dtype)
            start, at = start + size, at + len(chunk)

    shapes = [chunk[0].shape for chunk in parts]
    block = lambda shape: pl.BlockSpec((shape[0], rows), lambda i, s: (0, i))
    return call(
        kernel,
        (blocks,),
        [slots, summed, adapter_in] + flat,
        [
            pl.BlockSpec((twice, rows), lambda i, s: (0, i)),
            pl.BlockSpec((1, rank, units), lambda i, s: (s[i], 0, 0)),
        ]
        + [block(p.shape) for p in flat],
        [block(shape) for shape in shapes],
        [jax.ShapeDtypeStruct(shape, jnp.bfloat16) for shape in shapes],
        [],
        BIG,
    )


def finish(parts):
    flat = [p for chunk in parts for p in chunk]
    units = sum(chunk[0].shape[0] for chunk in parts)
    tokens = flat[0].shape[1]
    lanes = tokens // 2

    def kernel(*refs):
        start, at = 0, 0
        for chunk in parts:
            size = refs[at].shape[0]
            total = added(refs[at : at + len(chunk)], slice(None))
            refs[-1][start : start + size, :] = total.astype(refs[-1].dtype)
            start, at = start + size, at + len(chunk)

    return pl.pallas_call(
        kernel,
        grid=(tokens // lanes,),
        in_specs=[pl.BlockSpec((p.shape[0], lanes), lambda i: (0, i)) for p in flat],
        out_specs=pl.BlockSpec((units, lanes), lambda i: (0, i)),
        out_shape=jax.ShapeDtypeStruct((units, tokens), jnp.bfloat16),
        compiler_params=pltpu.CompilerParams(vmem_limit_bytes=20 * MIB),
        cost_estimate=pl.CostEstimate(flops=1000000, bytes_accessed=1000000, transcendentals=0),
    )(*flat)


def body(hidden, cotangent, down_weight, adapter_in, adapter_out, adapter_ids, adapter_slot):
    hidden = hidden.T
    units, tokens = hidden.shape
    x = lax.axis_index("x")
    z = lax.axis_index("z")
    slots = adapter_slot[adapter_ids[:, 0]]

    width = cotangent.shape[1] // 2
    turned = []
    for k in range(2):
        at = lax.rem(z + k, 2) * width
        piece = lax.dynamic_slice_in_dim(cotangent, at, width, axis=1)
        pairs = [
            (c * N + d, (d // 2) * N + 2 * c + (d + k) % 2) for c in range(2) for d in range(N)
        ]
        turned.append(lax.ppermute(piece, ("c", "z"), pairs))
    first = (units // 2 + 15) // 16 * 16
    own = [down_weight[:first], down_weight[first:]]
    after, before = [take_from(own[0], "x", 1)], [take_from(own[0], "x", -1)]

    barrier = lax.optimization_barrier
    summed = sum_over_dp(rank_sums(slots, cotangent, hidden, adapter_out, adapter_in))
    *turned, after[0], before[0], summed, own[1] = barrier(
        (*turned, after[0], before[0], summed, own[1])
    )
    gathered = lax.all_gather(packed(turned), ("y", "c")).reshape(N, 2, 2, tokens, width)
    after.append(take_from(own[1], "x", 1))
    before.append(take_from(own[1], "x", -1))
    index = jnp.concatenate([slots, x[None].astype(jnp.int32)])
    terms = gradient_terms(index, summed, cotangent, hidden, adapter_scale / math.sqrt(tokens))
    sums = lax.psum_scatter(terms, "z", scatter_dimension=0)
    after[0], after[1], before[1], terms = barrier((after[0], after[1], before[1], terms))
    fars = [take_from(after[0], "x", 1), take_from(before[1], "x", -1)]

    def make(chunk, *steps):
        index = jnp.stack([lax.rem(z + s, N) // 2 for s in steps] + [x]).astype(jnp.int32)
        weights = (own[chunk], after[chunk], fars[chunk], before[chunk])
        return products(index, gathered, weights, steps)

    far0, left0 = make(0, 2, 3)
    far1, right1 = make(1, 2, 1)
    right0, own0 = make(0, 1, 0)
    left1, own1 = make(1, 3, 0)
    parts = scatter_ring(far0, right0, left0, own0, "z", 1)
    parts += scatter_ring(far1, right1, left1, own1, "z", -1)
    own0, left0, right0, own1, left1, right1 = parts
    ready = early_sums(slots, summed, adapter_in, [[own0, left0], [own1]])
    sums = second_hop(sums, "x")
    *ready, sums[0] = barrier((*ready, sums[0]))
    hidden_gradient = finish([[ready[0], right0], [ready[1], left1, right1]])
    grad_in, grad_out = last_sum(sums, units, cotangent.shape[1])
    return hidden_gradient.T, grad_in, grad_out


def solution(mesh):
    fine = Mesh(mesh.devices.reshape(N, 2, N, N), ("y", "c", "x", "z"))
    dp, fsdp = ("y", "c"), ("x", "z")
    placed = (
        P(fsdp, dp),
        P(fsdp, dp),
        P(dp, fsdp),
        P(None, None, dp),
        P(None, None, dp),
        P(fsdp, None),
        P(),
    )
    return jax.shard_map(
        body,
        mesh=fine,
        in_specs=placed,
        out_specs=(P(fsdp, dp), P(fsdp, None, dp), P(fsdp, None, dp)),
        check_vma=False,
    )
```

```python
import math

import jax
import jax.numpy as jnp
from jax import lax
from jax.experimental import pallas as pl
from jax.experimental.pallas import tpu as pltpu
from jax.sharding import Mesh, PartitionSpec as P

adapter_scale = 2.0
N = 4
MIB = 1024 * 1024
BIG = 52
NN = (((1,), (0,)), ((), ()))
NT = (((1,), (1,)), ((), ()))
TN = (((0,), (0,)), ((), ()))


def take_from(array, axis, step):
    return lax.ppermute(array, axis, [((i + step) % N, i) for i in range(N)])


def other_core(array):
    return lax.ppermute(array, "c", [(0, 1), (1, 0)])


def sum_over_dp(array):
    array = array + other_core(array)
    array = array + lax.ppermute(array, "y", [(0, 1), (1, 0), (2, 3), (3, 2)])
    return array + lax.ppermute(array, "y", [(0, 3), (3, 0), (1, 2), (2, 1)])


def scatter_ring(far, right, left, own, axis, way):
    via = take_from(far, axis, -way)
    if way > 0:
        left = take_from(left, axis, 1)
        right = take_from(right + via, axis, -1)
    else:
        right = take_from(right, axis, -1)
        left = take_from(left + via, axis, 1)
    return [own, left, right]


def whole(array):
    return pl.BlockSpec(array.shape, lambda i, ix: (0,) * array.ndim)


def call(kernel, grid, operands, in_specs, out_specs, out_shape, scratch, mib):
    return pl.pallas_call(
        kernel,
        grid_spec=pltpu.PrefetchScalarGridSpec(
            num_scalar_prefetch=1,
            grid=grid,
            in_specs=in_specs,
            out_specs=out_specs,
            scratch_shapes=scratch,
        ),
        out_shape=out_shape,
        compiler_params=pltpu.CompilerParams(vmem_limit_bytes=mib * MIB),
        cost_estimate=pl.CostEstimate(flops=1000000, bytes_accessed=1000000, transcendentals=0),
    )(*operands)


def rank_sums(slots, cotangent, hidden, adapter_out, adapter_in):
    tokens, width = cotangent.shape
    units = hidden.shape[0]
    rank = adapter_in.shape[1]
    blocks = slots.shape[0]
    rows = tokens // blocks

    def kernel(slots, cotangent, hidden, a_out, a_in, out, cot, hid, outs, ins, sems):
        copies = [
            pltpu.make_async_copy(cotangent, cot, sems.at[0]),
            pltpu.make_async_copy(hidden, hid, sems.at[1]),
        ]
        for b in range(blocks):
            copies.append(pltpu.make_async_copy(a_out.at[slots[b]], outs.at[b], sems.at[2 + b]))
        for b in range(blocks):
            copies.append(
                pltpu.make_async_copy(a_in.at[slots[b]], ins.at[b], sems.at[2 + blocks + b])
            )
        for copy in copies:
            copy.start()
        for copy in copies:
            copy.wait()
        for b in range(blocks):
            at = slice(b * rows, (b + 1) * rows)
            out[:rank, at] = lax.dot_general(
                outs[b], cot[at, :], NT, preferred_element_type=jnp.float32
            ).astype(out.dtype)
            out[rank:, at] = lax.dot_general(
                ins[b], hid[:, at], NN, preferred_element_type=jnp.float32
            ).astype(out.dtype)

    far = pl.BlockSpec(memory_space=pltpu.HBM)
    return call(
        kernel,
        (1,),
        (slots, cotangent, hidden, adapter_out, adapter_in),
        [far] * 4,
        pl.BlockSpec(memory_space=pltpu.VMEM),
        jax.ShapeDtypeStruct((2 * rank, tokens), jnp.bfloat16),
        [
            pltpu.VMEM((tokens, width), jnp.bfloat16),
            pltpu.VMEM((units, tokens), jnp.bfloat16),
            pltpu.VMEM((blocks, rank, width), jnp.bfloat16),
            pltpu.VMEM((blocks, rank, units), jnp.bfloat16),
            pltpu.SemaphoreType.DMA((2 + 2 * blocks,)),
        ],
        BIG,
    )


def gradient_terms(index, summed, cotangent, hidden, multiplier):
    blocks = index.shape[0] - 1
    tokens, width = cotangent.shape
    rows = tokens // blocks
    units = hidden.shape[0]
    wide = width + units
    wide = wide + -wide % 128
    rank = summed.shape[0] // 2
    shape = (N, N, rank, wide)

    def kernel(index, summed, cotangent, hidden, out, products, staged, sems):
        for b in range(blocks):
            at = slice(b * rows, (b + 1) * rows)
            products[b, :, :width] = lax.dot_general(
                summed[rank:, at], cotangent[at, :], NN, preferred_element_type=jnp.float32
            )
            products[b, :, width : width + units] = lax.dot_general(
                summed[:rank, at], hidden[:, at], NT, preferred_element_type=jnp.float32
            )
            products[b, :, width + units :] = jnp.zeros((rank, wide - width - units), jnp.float32)
        x = index[blocks]
        staged[...] = jnp.zeros(staged.shape, staged.dtype)
        for b in range(blocks):
            total = jnp.float32(multiplier) * products[b]
            for other in range(blocks):
                if other != b:
                    same = jnp.where(index[other] == index[b], multiplier, 0.0)
                    total = total + same.astype(jnp.float32) * products[other]
            place = lax.rem(lax.div(index[b], N) - x + N, N)
            staged[lax.rem(index[b], N), place] = total.astype(staged.dtype)
        copies = []
        for s in range(N):
            copies.append(pltpu.make_async_copy(staged.at[s], out.at[s], sems.at[s]))
            copies[s].start()
        for copy in copies:
            copy.wait()

    return call(
        kernel,
        (1,),
        (index, summed, cotangent, hidden),
        [whole(a) for a in (summed, cotangent, hidden)],
        pl.BlockSpec(memory_space=pl.ANY),
        jax.ShapeDtypeStruct(shape, jnp.bfloat16),
        [
            pltpu.VMEM((blocks, rank, wide), jnp.float32),
            pltpu.VMEM(shape, jnp.bfloat16),
            pltpu.SemaphoreType.DMA((N,)),
        ],
        BIG,
    )


def second_hop(sums, axis):
    rank = sums.shape[0] // N
    parts = [sums[t * rank : (t + 1) * rank] for t in range(N)]
    return [parts[0]] + [take_from(parts[t], axis, -t) for t in range(1, N)]


def added(refs, at):
    total = refs[0][at, :].astype(jnp.float32)
    for ref in refs[1:]:
        total = total + ref[at, :].astype(jnp.float32)
    return total


def last_kernel(own, across, before, after, out_in, out_out):
    split, units = out_out.shape[2], out_in.shape[2]
    total = added((own, across, before, after), slice(None))
    out_out[0] = total[:, :split].astype(out_out.dtype)
    out_in[0] = total[:, split : split + units].astype(out_in.dtype)


def last_sum(parts, units, width):
    rank = parts[0].shape[0]
    return pl.pallas_call(
        last_kernel,
        out_shape=[jax.ShapeDtypeStruct((1, rank, n), jnp.bfloat16) for n in (units, width)],
        compiler_params=pltpu.CompilerParams(vmem_limit_bytes=6 * MIB),
        cost_estimate=pl.CostEstimate(flops=1000000, bytes_accessed=1000000, transcendentals=0),
    )(*parts)


def packed(pieces):
    rows, width = pieces[0].shape

    def kernel(*refs):
        for n, ref in enumerate(refs[:-1]):
            refs[-1][n] = ref[...]

    return pl.pallas_call(
        kernel,
        grid=(2,),
        in_specs=[pl.BlockSpec((rows // 2, width), lambda i: (i, 0))] * len(pieces),
        out_specs=pl.BlockSpec((len(pieces), rows // 2, width), lambda i: (0, i, 0)),
        out_shape=jax.ShapeDtypeStruct((len(pieces), rows, width), pieces[0].dtype),
        compiler_params=pltpu.CompilerParams(vmem_limit_bytes=BIG * MIB),
        cost_estimate=pl.CostEstimate(flops=1000000, bytes_accessed=1000000, transcendentals=0),
    )(*pieces)


def products(index, gathered, weights, steps):
    rows, width = weights[0].shape
    tokens = gathered.shape[3]

    def kernel(index, gathered, *refs):
        pieces, outs, held, sides, sems = refs[:N], refs[N : N + 2], refs[-3], refs[-2], refs[-1]
        copies = {}
        for n, step in enumerate(steps):
            for r in range(N):
                copies[n, r] = pltpu.make_async_copy(
                    gathered.at[lax.rem(index[2] + r, N), index[n], step % 2],
                    sides.at[n, r],
                    sems.at[n, r],
                )
                copies[n, r].start()
                if n == 0:
                    copies[2, r] = pltpu.make_async_copy(pieces[r], held.at[r], sems.at[2, r])
                    copies[2, r].start()
        for n in range(2):
            total = None
            for r in range(N):
                if n == 0:
                    copies[2, r].wait()
                copies[n, r].wait()
                part = lax.dot_general(
                    held[r], sides[n, r], NT, preferred_element_type=jnp.float32
                )
                total = part if total is None else total + part
            outs[n][...] = total.astype(jnp.bfloat16)

    shape = (rows, tokens)
    return call(
        kernel,
        (1,),
        [index, gathered, *weights],
        [pl.BlockSpec(memory_space=pltpu.HBM)] + [pl.BlockSpec(memory_space=pl.ANY)] * N,
        [pl.BlockSpec(memory_space=pltpu.VMEM)] * 2,
        [jax.ShapeDtypeStruct(shape, jnp.bfloat16)] * 2,
        [
            pltpu.VMEM((N, rows, width), jnp.bfloat16),
            pltpu.VMEM((2, N, tokens, width), jnp.bfloat16),
            pltpu.SemaphoreType.DMA((3, N)),
        ],
        BIG,
    )


def early_sums(slots, summed, adapter_in, parts):
    twice, tokens = summed.shape
    blocks = slots.shape[0]
    rows = tokens // blocks
    rank, units = adapter_in.shape[1:]
    flat = [p for chunk in parts for p in chunk]

    def kernel(slots, summed, a_in, *refs):
        low = adapter_scale * lax.dot_general(
            a_in[0], summed[:rank, :], TN, preferred_element_type=jnp.float32
        )
        start, at = 0, 0
        for chunk, out in zip(parts, refs[len(flat) :]):
            size = out.shape[0]
            total = low[start : start + size] + added(refs[at : at + len(chunk)], slice(None))
            out[...] = total.astype(out.dtype)
            start, at = start + size, at + len(chunk)

    shapes = [chunk[0].shape for chunk in parts]
    block = lambda shape: pl.BlockSpec((shape[0], rows), lambda i, s: (0, i))
    return call(
        kernel,
        (blocks,),
        [slots, summed, adapter_in] + flat,
        [
            pl.BlockSpec((twice, rows), lambda i, s: (0, i)),
            pl.BlockSpec((1, rank, units), lambda i, s: (s[i], 0, 0)),
        ]
        + [block(p.shape) for p in flat],
        [block(shape) for shape in shapes],
        [jax.ShapeDtypeStruct(shape, jnp.bfloat16) for shape in shapes],
        [],
        BIG,
    )


def finish(parts):
    flat = [p for chunk in parts for p in chunk]
    units = sum(chunk[0].shape[0] for chunk in parts)
    tokens = flat[0].shape[1]
    lanes = tokens // 2

    def kernel(*refs):
        start, at = 0, 0
        for chunk in parts:
            size = refs[at].shape[0]
            total = added(refs[at : at + len(chunk)], slice(None))
            refs[-1][start : start + size, :] = total.astype(refs[-1].dtype)
            start, at = start + size, at + len(chunk)

    return pl.pallas_call(
        kernel,
        grid=(tokens // lanes,),
        in_specs=[pl.BlockSpec((p.shape[0], lanes), lambda i: (0, i)) for p in flat],
        out_specs=pl.BlockSpec((units, lanes), lambda i: (0, i)),
        out_shape=jax.ShapeDtypeStruct((units, tokens), jnp.bfloat16),
        compiler_params=pltpu.CompilerParams(vmem_limit_bytes=20 * MIB),
        cost_estimate=pl.CostEstimate(flops=1000000, bytes_accessed=1000000, transcendentals=0),
    )(*flat)


def body(hidden, cotangent, down_weight, adapter_in, adapter_out, adapter_ids, adapter_slot):
    hidden = hidden.T
    units, tokens = hidden.shape
    x = lax.axis_index("x")
    z = lax.axis_index("z")
    slots = adapter_slot[adapter_ids[:, 0]]

    width = cotangent.shape[1] // 2
    turned = []
    for k in range(2):
        at = lax.rem(z + k, 2) * width
        piece = lax.dynamic_slice_in_dim(cotangent, at, width, axis=1)
        pairs = [
            (c * N + d, (d // 2) * N + 2 * c + (d + k) % 2) for c in range(2) for d in range(N)
        ]
        turned.append(lax.ppermute(piece, ("c", "z"), pairs))
    first = (units // 2 + 15) // 16 * 16
    own = [down_weight[:first], down_weight[first:]]
    after, before = [take_from(own[0], "x", 1)], [take_from(own[0], "x", -1)]

    barrier = lax.optimization_barrier
    summed = sum_over_dp(rank_sums(slots, cotangent, hidden, adapter_out, adapter_in))
    *turned, after[0], before[0], summed, own[1] = barrier(
        (*turned, after[0], before[0], summed, own[1])
    )
    gathered = lax.all_gather(packed(turned), ("y", "c")).reshape(N, 2, 2, tokens, width)
    after.append(take_from(own[1], "x", 1))
    before.append(take_from(own[1], "x", -1))
    index = jnp.concatenate([slots, x[None].astype(jnp.int32)])
    terms = gradient_terms(index, summed, cotangent, hidden, adapter_scale / math.sqrt(tokens))
    terms = terms.reshape(N, -1, terms.shape[3])
    sums = lax.psum_scatter(terms, "z", scatter_dimension=0)
    after[0], after[1], before[1], terms = barrier((after[0], after[1], before[1], terms))
    fars = [take_from(after[0], "x", 1), take_from(before[1], "x", -1)]

    def make(chunk, *steps):
        index = jnp.stack([lax.rem(z + s, N) // 2 for s in steps] + [x]).astype(jnp.int32)
        weights = (own[chunk], after[chunk], fars[chunk], before[chunk])
        return products(index, gathered, weights, steps)

    far0, left0 = make(0, 2, 3)
    far1, right1 = make(1, 2, 1)
    right0, own0 = make(0, 1, 0)
    left1, own1 = make(1, 3, 0)
    parts = scatter_ring(far0, right0, left0, own0, "z", 1)
    parts += scatter_ring(far1, right1, left1, own1, "z", -1)
    own0, left0, right0, own1, left1, right1 = parts
    ready = early_sums(slots, summed, adapter_in, [[own0, left0], [own1]])
    sums = second_hop(sums, "x")
    *ready, sums[0] = barrier((*ready, sums[0]))
    hidden_gradient = finish([[ready[0], right0], [ready[1], left1, right1]])
    grad_in, grad_out = last_sum(sums, units, cotangent.shape[1])
    return hidden_gradient.T, grad_in, grad_out


def solution(mesh):
    fine = Mesh(mesh.devices.reshape(N, 2, N, N), ("y", "c", "x", "z"))
    dp, fsdp = ("y", "c"), ("x", "z")
    placed = (
        P(fsdp, dp),
        P(fsdp, dp),
        P(dp, fsdp),
        P(None, None, dp),
        P(None, None, dp),
        P(fsdp, None),
        P(),
    )
    return jax.shard_map(
        body,
        mesh=fine,
        in_specs=placed,
        out_specs=(P(fsdp, dp), P(fsdp, None, dp), P(fsdp, None, dp)),
        check_vma=False,
    )
```
